256 devices in a mesh: seq: 32 (over z, x), row: 2 (over core), col: 4 (over y).
Axes of the slice: x: 4, y: 4, z: 8, core: 2. Of those that a mesh axis runs over, the one named last changes fastest.
Arguments:
- query_proj: bfloat16 [9216, 4096], P('seq', ('row', 'col')), may hold values from -6 to 6
- key_proj: bfloat16 [9216, 4096], P('seq', ('row', 'col')), may hold values from -6 to 6
- value_proj: bfloat16 [9216, 4096], P('seq', ('row', 'col')), may hold values from -6 to 6
- query_gain: float32 [4096], P(('row', 'col')), may hold values from 1 to 6.4
- key_gain: float32 [4096], P(('row', 'col')), may hold values from 1 to 6.4
- residual: bfloat16 [9216, 6144], P(('seq', 'row'), 'col'), may hold values from -6 to 6
- out_weight: bfloat16 [4096, 6144], P('row', 'col'), may hold values from -0.09375 to 0.09375
Outputs:
- block_out: bfloat16 [9216, 6144], P(('seq', 'row'), 'col')
The draws below stay inside these ranges and needn't reach their ends.
All inputs are finite; a program needn't handle non-finite values.
Results may differ from the reference program's by a relative error of at most 0.012.
Values may be sent and summed in bfloat16 or wider, within the bound.
No kernel may reach another device: no remote copies, remote signals or barrier semaphores. Data moves between devices by JAX's collectives and lax.ppermute only.
A program may use at most 192 MiB of HBM per device.

```python
import math
import jax
import jax.numpy as jnp
from jax import lax

D = 6144
H = 32
DH = 128
HD = 4096
TOKENS = 9216


def shared_base(key):
    return jax.random.truncated_normal(jax.random.fold_in(key, 77), -6.0, 6.0, (TOKENS, HD), jnp.float32)


def head_strength(key, top):
    uniform_draw = jax.random.uniform(jax.random.fold_in(key, 101), (H,), jnp.float32)
    return jnp.exp(uniform_draw * jnp.log(top))


def gain_from(key, top):
    strength = head_strength(key, top)
    head_index = jnp.arange(HD) // DH
    factor = jax.random.uniform(key, (HD,), jnp.float32, 1.0, 2.0)
    return strength[head_index] * factor


def draw_query_proj(key, part):
    key = jax.random.fold_in(key, 1)
    own_rows = jax.random.truncated_normal(key, -6.0, 6.0, (TOKENS, HD), jnp.float32)
    return own_rows.astype(jnp.bfloat16)


def draw_key_proj(key, part):
    base = shared_base(key)
    return base.astype(jnp.bfloat16)


def draw_query_gain(key, part):
    inner = jax.random.fold_in(key, 3)
    return gain_from(inner, 1.0)


def draw_key_gain(key, part):
    inner = jax.random.fold_in(key, 4)
    return gain_from(inner, 1.0)


def block_levels(rng, shape, split, low, largest):
    level = 1.0
    for position, blocks in split:
        draws = jax.random.uniform(jax.random.fold_in(jax.random.fold_in(rng, 6), position), (blocks,), jnp.float32, low / len(split), largest / len(split))
        level = level * jnp.repeat(jnp.exp(draws), shape[position] // blocks).reshape((-1,) + (1,) * (len(shape) - 1 - position))
    return level


def gaussian(key, shape, spread, limit, cuts=(), held_as=jnp.bfloat16):
    values = jax.random.normal(key, shape, jnp.float32) * spread
    if len(cuts) > 0:
        values = block_levels(key, shape, cuts, -0.22, 0.18) * values
    return jnp.clip(values, min=-limit, max=limit).astype(held_as)


def setup_inputs(seed: int = 0) -> dict:
    seeds = jax.random.split(jax.random.key(seed), 8)
    query_proj = draw_query_proj(jax.random.fold_in(seeds[7], 71), 0)
    key_proj = draw_key_proj(jax.random.fold_in(seeds[7], 71), 0)
    value_proj = gaussian(seeds[2], (TOKENS, HD), 1.0, 6.0, ((0, 32), (1, 8)))
    query_gain = draw_query_gain(jax.random.fold_in(seeds[7], 71), 0)
    key_gain = draw_key_gain(jax.random.fold_in(seeds[7], 71), 0)
    residual = gaussian(seeds[5], (TOKENS, D), 1.0, 6.0, ((0, 64), (1, 4)))
    out_weight = gaussian(seeds[6], (HD, D), HD ** -0.5, 0.09375, ((0, 2), (1, 4)))
    return dict(query_proj=query_proj, key_proj=key_proj, value_proj=value_proj, query_gain=query_gain, key_gain=key_gain, residual=residual, out_weight=out_weight)


epsilon = 1e-06

def normalize(values, gain_values):
    centre = lax.optimization_barrier(jnp.mean(values, axis=-1, keepdims=True))
    shifted = values - centre
    variance = lax.optimization_barrier(jnp.mean(shifted * shifted, axis=-1, keepdims=True))
    return shifted * lax.rsqrt(variance + epsilon) * gain_values

def one_head(operands):
    query_head, key_head, value_head = operands
    scores = jnp.dot(query_head, key_head.T, preferred_element_type=jnp.float32)
    highest = lax.optimization_barrier(jnp.max(scores, axis=1, keepdims=True))
    weights = jnp.exp(scores - highest)
    denominator = lax.optimization_barrier(jnp.sum(weights, axis=1, keepdims=True))
    summed = jnp.dot(weights.astype(jnp.bfloat16), value_head, preferred_element_type=jnp.float32)
    return (summed / denominator).astype(jnp.bfloat16)

def reference(query_proj, key_proj, value_proj, query_gain, key_gain, residual, out_weight):
    factor = 1.0 / math.sqrt(DH)
    queries = normalize(query_proj.astype(jnp.float32).reshape(TOKENS, H, DH), query_gain.reshape(H, DH))
    queries = (queries * factor).astype(jnp.bfloat16)
    normed = normalize(key_proj.astype(jnp.float32).reshape(TOKENS, H, DH), key_gain.reshape(H, DH))
    normed = normed.astype(jnp.bfloat16)
    value_heads = value_proj.reshape(TOKENS, H, DH)
    attended = lax.map(one_head, (jnp.transpose(queries, (1, 0, 2)), jnp.transpose(normed, (1, 0, 2)), jnp.transpose(value_heads, (1, 0, 2))))
    attended = jnp.transpose(attended, (1, 0, 2)).reshape(TOKENS, H * DH)
    product = jnp.dot(attended, out_weight, preferred_element_type=jnp.float32)
    return (residual.astype(jnp.float32) + product).astype(jnp.bfloat16)
```

```python
import functools
import math

import jax
import jax.numpy as jnp
from jax import lax
from jax.experimental import pallas as pl
from jax.experimental.pallas import tpu as pltpu
from jax.sharding import Mesh, PartitionSpec as P

DH = 128
EPS = 1e-06
BF = jnp.bfloat16
F32 = jnp.float32
NZ, NX, NC, NY = 8, 4, 2, 4
ROWS = 288
HEADS = 4
GROUPS = ((0, 2), (1, 3))
NT = (((1,), (1,)), ((), ()))
SMEM = pltpu.MemorySpace.SMEM
VLIM = 48 << 20


def norm(values, gain):
    centre = jnp.mean(values, axis=-1, keepdims=True)
    shifted = values - centre
    variance = jnp.mean(shifted * shifted, axis=-1, keepdims=True)
    return shifted * lax.rsqrt(variance + EPS) * gain


def norm_kernel(turn_ref, q_ref, k_ref, v_ref, qg_ref, kg_ref, *outs):
    for j in range(HEADS):
        head = lax.rem(turn_ref[0] + j, HEADS)
        cols = pl.ds(pl.multiple_of(head * DH, DH), DH)
        outs[j][:, :DH] = norm(k_ref[:, cols].astype(F32), kg_ref[:, cols]).astype(BF)
        outs[j][:, DH:] = v_ref[:, cols]
        queries = norm(q_ref[:, cols].astype(F32), qg_ref[:, cols])
        outs[HEADS + j][...] = (queries * (1.0 / math.sqrt(DH))).astype(BF)


def flash_kernel(first, last, nkv, kb, *refs):
    queries, refs = refs[:HEADS], refs[HEADS:]
    pieces, refs = refs[:nkv], refs[nkv:]
    if not first:
        (acc_in, max_in, sum_in), refs = refs[:3], refs[3:]
    if last:
        outs, refs = refs[:HEADS], refs[HEADS:]
    else:
        outs, refs = refs[:3], refs[3:]
    kv, sem = refs
    piece = pieces[0].shape[0]
    copies = [
        pltpu.make_async_copy(pieces[i], kv.at[pl.ds(i * piece, piece)], sem.at[i])
        for i in range(nkv)
    ]
    for c in copies:
        c.start()
    for c in copies:
        c.wait()
    blocks = kv.shape[0] // kb
    for i in range(HEADS):
        rows = slice(i * ROWS, (i + 1) * ROWS)
        q = queries[i][...]

        def scores(b):
            return lax.dot_general(
                q, kv[b * kb : (b + 1) * kb, :DH], NT, preferred_element_type=F32
            )

        if first:
            high = None
        else:
            high, total, acc = max_in[rows, :1], sum_in[rows, :1], acc_in[rows, :]
        ahead = scores(0)
        for b in range(blocks):
            s = ahead
            if b + 1 < blocks:
                ahead = scores(b + 1)
            top = jnp.max(s, axis=1, keepdims=True)
            top = top if high is None else jnp.maximum(high, top)
            p = jnp.exp(s - top).astype(BF)
            v = kv[b * kb : (b + 1) * kb, DH:]
            both = jnp.dot(
                p, jnp.concatenate([v, jnp.ones_like(v)], axis=1), preferred_element_type=F32
            )
            part, psum = both[:, :DH], both[:, DH : DH + 1]
            if high is None:
                acc, total = part, psum
            else:
                scale = jnp.exp(high - top)
                acc, total = acc * scale + part, total * scale + psum
            high = top
        if last:
            outs[i][...] = (acc / total).astype(BF)
        else:
            outs[0][rows, :] = acc
            outs[1][rows, :] = jnp.broadcast_to(high, (ROWS, DH))
            outs[2][rows, :] = jnp.broadcast_to(total, (ROWS, DH))


def flash(first, last, queries, pieces, state):
    n = len(pieces)
    keys = n * pieces[0].shape[0]
    nq = HEADS * ROWS
    if last:
        shapes = [jax.ShapeDtypeStruct((ROWS, DH), BF)] * HEADS
    else:
        shapes = [jax.ShapeDtypeStruct((nq, DH), F32)] * 3
    vm = pl.BlockSpec(memory_space=pltpu.VMEM)
    return pl.pallas_call(
        functools.partial(flash_kernel, first, last, n, 1536),
        out_shape=shapes,
        in_specs=[vm] * HEADS + [pl.BlockSpec(memory_space=pl.ANY)] * n + [vm] * len(state),
        out_specs=[vm] * len(shapes),
        scratch_shapes=[pltpu.VMEM((keys, 2 * DH), BF), pltpu.SemaphoreType.DMA((n,))],
        compiler_params=pltpu.CompilerParams(vmem_limit_bytes=VLIM),
        cost_estimate=pl.CostEstimate(
            flops=8 * nq * keys * DH, bytes_accessed=keys * 512 + nq * 256, transcendentals=nq * keys
        ),
    )(*queries, *pieces, *state)


def project_kernel(pos_ref, *refs):
    blocks, (w_ref, keep_ref, send_ref, tokens) = refs[:NY], refs[NY:]
    turn, col, core = pos_ref[0], pos_ref[1], pos_ref[2]
    for s in range(NY):
        source = lax.rem(col + NY - s, NY)
        for j in range(HEADS):
            head = lax.rem(turn + j, HEADS)
            cols = pl.ds(pl.multiple_of(source * (HEADS * DH) + head * DH, DH), DH)
            tokens[:, cols] = blocks[s][:, j * DH : (j + 1) * DH]
    half = ROWS // 2
    for mine in range(2):
        start = (core if mine else 1 - core) * half
        part = tokens[pl.ds(pl.multiple_of(start, 16), half), :]
        out = jnp.dot(part, w_ref[...], preferred_element_type=F32)
        if mine:
            keep_ref[...] = out
        else:
            send_ref[...] = out


def project(pos, blocks, weight):
    vm = pl.BlockSpec(memory_space=pltpu.VMEM)
    half = ROWS // 2
    n = weight.shape[1]
    return pl.pallas_call(
        project_kernel,
        out_shape=[jax.ShapeDtypeStruct((half, n), F32)] * 2,
        in_specs=[pl.BlockSpec(memory_space=SMEM)] + [vm] * (NY + 1),
        out_specs=[vm] * 2,
        scratch_shapes=[pltpu.VMEM((ROWS, weight.shape[0]), BF)],
        compiler_params=pltpu.CompilerParams(vmem_limit_bytes=VLIM),
    )(pos, *blocks, weight)


def norms(turn, q, k, v, qg, kg):
    vm = pl.BlockSpec(memory_space=pltpu.VMEM)
    return pl.pallas_call(
        norm_kernel,
        out_shape=[jax.ShapeDtypeStruct((ROWS, 2 * DH), BF)] * HEADS
        + [jax.ShapeDtypeStruct((ROWS, DH), BF)] * HEADS,
        in_specs=[pl.BlockSpec(memory_space=SMEM)] + [vm] * 5,
        out_specs=[vm] * (2 * HEADS),
        compiler_params=pltpu.CompilerParams(vmem_limit_bytes=VLIM),
    )(turn, q, k, v, qg, kg)


def out_perm(j):
    return [
        (z * NC + c, (HEADS * c + (j + z // 2) % HEADS) * NC + z % 2)
        for z in range(NZ)
        for c in range(NC)
    ]


def to_owner(value, j):
    return lax.ppermute(value, ("z", "row"), out_perm(j))


def from_owner(value, j):
    return lax.ppermute(value, ("z", "row"), [(b, a) for a, b in out_perm(j)])


def shift(value, axis, size, step):
    return lax.ppermute(value, axis, [(i, (i + step) % size) for i in range(size)])


def swap(value):
    return lax.ppermute(value, "row", [(0, 1), (1, 0)])


def body(query_proj, key_proj, value_proj, query_gain, key_gain, residual, out_weight):
    turn = lax.axis_index("z") // 2
    pos = jnp.stack([turn, lax.axis_index("col"), lax.axis_index("row")]).astype(jnp.int32)
    outs = norms(
        pos, query_proj, key_proj, value_proj, query_gain.reshape(1, -1), key_gain.reshape(1, -1)
    )
    gathered = []
    for group in GROUPS:
        own = jnp.concatenate([to_owner(outs[j], j) for j in group], axis=0)
        held = [own] + [shift(own, "x", NX, s) for s in (1, -1, 2)]
        gathered.append(held + [swap(h) for h in held])
    queries = [to_owner(outs[HEADS + j], j) for j in range(HEADS)]
    state = flash(True, False, queries, gathered[0], ())
    attended = flash(False, True, queries, gathered[1], state)
    mine = jnp.concatenate([from_owner(attended[j], j) for j in range(HEADS)], axis=1)
    blocks = [mine] + [shift(mine, "col", NY, s) for s in (1, 2, 3)]
    keep, send = project(pos, blocks, out_weight)
    return (residual.astype(F32) + (keep + swap(send))).astype(BF)


def solution(mesh):
    fine = Mesh(mesh.devices.reshape(NZ, NX, NC, NY), ("z", "x", "row", "col"))
    seq = ("z", "x")
    heads = ("row", "col")
    placed = (
        P(seq, heads),
        P(seq, heads),
        P(seq, heads),
        P(heads),
        P(heads),
        P(("z", "x", "row"), "col"),
        P("row", "col"),
    )
    return jax.shard_map(
        body, mesh=fine, in_specs=placed, out_specs=P(("z", "x", "row"), "col"), check_vma=False
    )
```

```python
import functools
import math

import jax
import jax.numpy as jnp
from jax import lax
from jax.experimental import pallas as pl
from jax.experimental.pallas import tpu as pltpu
from jax.sharding import Mesh, PartitionSpec as P

DH = 128
EPS = 1e-06
BF = jnp.bfloat16
F32 = jnp.float32
NZ, NX, NC, NY = 8, 4, 2, 4
ROWS = 288
HEADS = 4
NT = (((1,), (1,)), ((), ()))
SMEM = pltpu.MemorySpace.SMEM
VLIM = 48 << 20


def norm(values, gain):
    centre = jnp.mean(values, axis=-1, keepdims=True)
    shifted = values - centre
    variance = jnp.mean(shifted * shifted, axis=-1, keepdims=True)
    return shifted * lax.rsqrt(variance + EPS) * gain


def fetch(sources, held, sems):
    copies = [pltpu.make_async_copy(a, b, sems.at[i]) for i, (a, b) in enumerate(zip(sources, held))]
    for c in copies:
        c.start()
    for c in copies:
        c.wait()


def head_columns(turn_ref, j):
    head = lax.rem(turn_ref[0] + j, HEADS)
    return pl.ds(pl.multiple_of(head * DH, DH), DH)


def key_kernel(turn_ref, k_hbm, v_hbm, g_hbm, *refs):
    outs, (k_ref, v_ref, g_ref, sems) = refs[:HEADS], refs[HEADS:]
    fetch((k_hbm, v_hbm, g_hbm), (k_ref, v_ref, g_ref), sems)
    for j in range(HEADS):
        cols = head_columns(turn_ref, j)
        outs[j][:, :DH] = norm(k_ref[:, cols].astype(F32), g_ref[:, cols]).astype(BF)
        outs[j][:, DH:] = v_ref[:, cols]


def query_kernel(turn_ref, q_hbm, g_hbm, *refs):
    outs, (q_ref, g_ref, sems) = refs[:HEADS], refs[HEADS:]
    fetch((q_hbm, g_hbm), (q_ref, g_ref), sems)
    for j in range(HEADS):
        cols = head_columns(turn_ref, j)
        queries = norm(q_ref[:, cols].astype(F32), g_ref[:, cols])
        outs[j][...] = (queries * (1.0 / math.sqrt(DH))).astype(BF)


def norm_call(kernel, width, turn, *arrays):
    return pl.pallas_call(
        kernel,
        out_shape=[jax.ShapeDtypeStruct((ROWS, width), BF)] * HEADS,
        in_specs=[pl.BlockSpec(memory_space=SMEM)]
        + [pl.BlockSpec(memory_space=pltpu.MemorySpace.HBM)] * len(arrays),
        out_specs=[pl.BlockSpec(memory_space=pltpu.VMEM)] * HEADS,
        scratch_shapes=[pltpu.VMEM(a.shape, a.dtype) for a in arrays]
        + [pltpu.SemaphoreType.DMA((len(arrays),))],
        compiler_params=pltpu.CompilerParams(vmem_limit_bytes=VLIM),
    )(turn, *arrays)


def flash_kernel(first, last, nkv, kb, *refs):
    queries, refs = refs[:HEADS], refs[HEADS:]
    pieces, refs = refs[:nkv], refs[nkv:]
    if not first:
        (acc_in, max_in, sum_in), refs = refs[:3], refs[3:]
    if last:
        outs, refs = refs[:HEADS], refs[HEADS:]
    else:
        outs, refs = refs[:3], refs[3:]
    kv, sem = refs
    piece = pieces[0].shape[0]
    copies = [
        pltpu.make_async_copy(pieces[i], kv.at[pl.ds(i * piece, piece)], sem.at[i])
        for i in range(nkv)
    ]
    for c in copies:
        c.start()
    for c in copies:
        c.wait()
    blocks = kv.shape[0] // kb
    for i in range(HEADS):
        rows = slice(i * ROWS, (i + 1) * ROWS)
        q = queries[i][...]

        def scores(b):
            return lax.dot_general(
                q, kv[b * kb : (b + 1) * kb, :DH], NT, preferred_element_type=F32
            )

        if first:
            high = None
        else:
            high, total, acc = max_in[rows, :1], sum_in[rows, :1], acc_in[rows, :]
        ahead = scores(0)
        for b in range(blocks):
            s = ahead
            if b + 1 < blocks:
                ahead = scores(b + 1)
            top = jnp.max(s, axis=1, keepdims=True)
            top = top if high is None else jnp.maximum(high, top)
            p = jnp.exp(s - top).astype(BF)
            v = kv[b * kb : (b + 1) * kb, DH:]
            both = jnp.dot(
                p, jnp.concatenate([v, jnp.ones_like(v)], axis=1), preferred_element_type=F32
            )
            part, psum = both[:, :DH], both[:, DH : DH + 1]
            if high is None:
                acc, total = part, psum
            else:
                scale = jnp.exp(high - top)
                acc, total = acc * scale + part, total * scale + psum
            high = top
        if last:
            outs[i][...] = (acc / total).astype(BF)
        else:
            outs[0][rows, :] = acc
            outs[1][rows, :] = jnp.broadcast_to(high, (ROWS, DH))
            outs[2][rows, :] = jnp.broadcast_to(total, (ROWS, DH))


def flash(first, last, queries, pieces, state):
    n = len(pieces)
    keys = n * pieces[0].shape[0]
    nq = HEADS * ROWS
    if last:
        shapes = [jax.ShapeDtypeStruct((ROWS, DH), BF)] * HEADS
    else:
        shapes = [jax.ShapeDtypeStruct((nq, DH), F32)] * 3
    vm = pl.BlockSpec(memory_space=pltpu.VMEM)
    return pl.pallas_call(
        functools.partial(flash_kernel, first, last, n, 1152),
        out_shape=shapes,
        in_specs=[vm] * HEADS + [pl.BlockSpec(memory_space=pl.ANY)] * n + [vm] * len(state),
        out_specs=[vm] * len(shapes),
        scratch_shapes=[pltpu.VMEM((keys, 2 * DH), BF), pltpu.SemaphoreType.DMA((n,))],
        compiler_params=pltpu.CompilerParams(vmem_limit_bytes=VLIM),
        cost_estimate=pl.CostEstimate(flops=1000, bytes_accessed=1000, transcendentals=0),
    )(*queries, *pieces, *state)


def project_kernel(pos_ref, *refs):
    blocks, (w_ref, keep_ref, send_ref, tokens) = refs[:NY], refs[NY:]
    turn, col, core = pos_ref[0], pos_ref[1], pos_ref[2]
    half = ROWS // 2
    for s in range(NY):
        source = lax.rem(col + NY - s, NY)
        for j in range(HEADS):
            head = lax.rem(turn + j, HEADS)
            cols = pl.ds(pl.multiple_of(source * (HEADS * DH) + head * DH, DH), DH)
            for i in range(2):
                rows = pl.ds(pl.multiple_of(lax.rem(core + i, 2) * half, 16), half)
                tokens[i * half : (i + 1) * half, cols] = blocks[s][rows, j * DH : (j + 1) * DH]
    width = w_ref.shape[1]
    step = width // 3
    for n in range(0, width, step):
        out = jnp.dot(tokens[...], w_ref[:, n : n + step], preferred_element_type=F32)
        keep_ref[:, n : n + step] = out[:half]
        send_ref[:, n : n + step] = out[half:]


def project(pos, blocks, weight):
    vm = pl.BlockSpec(memory_space=pltpu.VMEM)
    half = ROWS // 2
    n = weight.shape[1]
    return pl.pallas_call(
        project_kernel,
        out_shape=[jax.ShapeDtypeStruct((half, n), F32)] * 2,
        in_specs=[pl.BlockSpec(memory_space=SMEM)] + [vm] * (NY + 1),
        out_specs=[vm] * 2,
        scratch_shapes=[pltpu.VMEM((ROWS, weight.shape[0]), BF)],
        compiler_params=pltpu.CompilerParams(vmem_limit_bytes=VLIM),
    )(pos, *blocks, weight)


def out_perm(j):
    return [
        (z * NC + c, (HEADS * c + (j + z // 2) % HEADS) * NC + z % 2)
        for z in range(NZ)
        for c in range(NC)
    ]


def to_owner(value, j):
    return lax.ppermute(value, ("z", "row"), out_perm(j))


def from_owner(value, j):
    return lax.ppermute(value, ("z", "row"), [(b, a) for a, b in out_perm(j)])


def shift(value, axis, size, step):
    return lax.ppermute(value, axis, [(i, (i + step) % size) for i in range(size)])


def swap(value):
    return lax.ppermute(value, "row", [(0, 1), (1, 0)])


def body(query_proj, key_proj, value_proj, query_gain, key_gain, residual, out_weight):
    turn = lax.axis_index("z") // 2
    pos = jnp.stack([turn, lax.axis_index("col"), lax.axis_index("row")]).astype(jnp.int32)
    keyed = norm_call(key_kernel, 2 * DH, pos, key_proj, value_proj, key_gain.reshape(1, -1))
    normed = norm_call(query_kernel, DH, pos, query_proj, query_gain.reshape(1, -1))
    arrived = [to_owner(keyed[j], j) for j in range(HEADS)]
    own = jnp.concatenate(arrived, axis=0)
    *normed, _ = lax.optimization_barrier((*normed, own))
    far, near, back = [shift(own, "x", NX, s) for s in (2, 1, -1)]
    queries = [to_owner(normed[j], j) for j in range(HEADS)]
    state = flash(True, False, queries, [own, swap(own)], ())
    near, back, *state = lax.optimization_barrier((near, back, *state))
    state = flash(False, False, queries, [near, back, swap(near), swap(back)], state)
    far, *state = lax.optimization_barrier((far, *state))
    attended = flash(False, True, queries, [far, swap(far)], state)
    mine = jnp.concatenate([from_owner(attended[j], j) for j in range(HEADS)], axis=1)
    blocks = [mine] + [shift(mine, "col", NY, s) for s in (1, 2, 3)]
    keep, send = project(pos, blocks, out_weight)
    return (residual.astype(F32) + (keep + swap(send))).astype(BF)


def solution(mesh):
    fine = Mesh(mesh.devices.reshape(NZ, NX, NC, NY), ("z", "x", "row", "col"))
    seq = ("z", "x")
    heads = ("row", "col")
    placed = (
        P(seq, heads),
        P(seq, heads),
        P(seq, heads),
        P(heads),
        P(heads),
        P(("z", "x", "row"), "col"),
        P("row", "col"),
    )
    return jax.shard_map(
        body, mesh=fine, in_specs=placed, out_specs=P(("z", "x", "row"), "col"), check_vma=False
    )
```

```python
import functools
import math

import jax
import jax.numpy as jnp
from jax import lax
from jax.experimental import pallas as pl
from jax.experimental.pallas import tpu as pltpu
from jax.sharding import Mesh, PartitionSpec as P

DH = 128
EPS = 1e-06
BF = jnp.bfloat16
F32 = jnp.float32
NZ, NX, NC, NY = 8, 4, 2, 4
ROWS = 288
HALF = ROWS // 2
HEADS = 4
NT = (((1,), (1,)), ((), ()))
VM = pl.BlockSpec(memory_space=pltpu.VMEM)
SM = pl.BlockSpec(memory_space=pltpu.MemorySpace.SMEM)
ANY = pl.BlockSpec(memory_space=pl.ANY)
VLIM = 40 << 20


def norm(values, gain):
    centre = jnp.mean(values, axis=-1, keepdims=True)
    shifted = values - centre
    variance = jnp.mean(shifted * shifted, axis=-1, keepdims=True)
    return shifted * lax.rsqrt(variance + EPS) * gain


def norm_kernel(pos_ref, *refs):
    sources, outs, held, sems = refs[:5], refs[5:9], refs[9:14], refs[14]
    copies = [
        pltpu.make_async_copy(a, b, sems.at[i]) for i, (a, b) in enumerate(zip(sources, held))
    ]
    for c in copies:
        c.start()
    k_ref, kg_ref, v_ref, q_ref, qg_ref = held
    heads = [lax.rem(pos_ref[0] + j, HEADS) for j in range(HEADS)]
    columns = [pl.ds(pl.multiple_of(h * DH, DH), DH) for h in heads]
    copies[0].wait()
    copies[1].wait()
    for out, cols in zip(outs, columns):
        out[:, :DH] = norm(k_ref[:, cols].astype(F32), kg_ref[:, cols]).astype(BF)
    copies[2].wait()
    for out, cols in zip(outs, columns):
        out[:, DH : 2 * DH] = v_ref[:, cols]
    copies[3].wait()
    copies[4].wait()
    for out, cols in zip(outs, columns):
        queries = norm(q_ref[:, cols].astype(F32), qg_ref[:, cols])
        out[:, 2 * DH :] = (queries * (1.0 / math.sqrt(DH))).astype(BF)


def norms(pos, *arrays):
    return pl.pallas_call(
        norm_kernel,
        out_shape=[jax.ShapeDtypeStruct((ROWS, 3 * DH), BF)] * HEADS,
        in_specs=[SM] + [ANY] * 5,
        out_specs=[VM] * HEADS,
        scratch_shapes=[pltpu.VMEM(a.shape, a.dtype) for a in arrays]
        + [pltpu.SemaphoreType.DMA((5,))],
        compiler_params=pltpu.CompilerParams(vmem_limit_bytes=62 << 20),
    )(pos, *arrays)


def flash_kernel(first, last, nkv, kb, *refs):
    queries, refs = refs[:HEADS], refs[HEADS:]
    pieces, refs = refs[:nkv], refs[nkv:]
    if not first:
        (acc_in, max_in, sum_in), refs = refs[:3], refs[3:]
    if last:
        outs, refs = refs[:HEADS], refs[HEADS:]
    else:
        outs, refs = refs[:3], refs[3:]
    kv, sem = refs
    piece = pieces[0].shape[0]
    copies = [
        pltpu.make_async_copy(pieces[i], kv.at[pl.ds(i * piece, piece)], sem.at[i])
        for i in range(nkv)
    ]
    for c in copies:
        c.start()
    for c in copies:
        c.wait()
    blocks = kv.shape[0] // kb
    for i in range(HEADS):
        rows = slice(i * ROWS, (i + 1) * ROWS)
        q = queries[i][:, 2 * DH :]

        def scores(b):
            return lax.dot_general(
                q, kv[b * kb : (b + 1) * kb, :DH], NT, preferred_element_type=F32
            )

        if first:
            high = None
        else:
            high, total, acc = max_in[rows, :1], sum_in[rows, :1], acc_in[rows, :]
        ahead = scores(0)
        for b in range(blocks):
            s = ahead
            if b + 1 < blocks:
                ahead = scores(b + 1)
            top = jnp.max(s, axis=1, keepdims=True)
            top = top if high is None else jnp.maximum(high, top)
            p = jnp.exp(s - top).astype(BF)
            v = kv[b * kb : (b + 1) * kb, DH:]
            both = jnp.dot(
                p, jnp.concatenate([v, jnp.ones_like(v)], axis=1), preferred_element_type=F32
            )
            part, psum = both[:, :DH], both[:, DH : DH + 1]
            if high is None:
                acc, total = part, psum
            else:
                scale = jnp.exp(high - top)
                acc, total = acc * scale + part, total * scale + psum
            high = top
        if last:
            outs[i][...] = (acc / total).astype(BF)
        else:
            outs[0][rows, :] = acc
            outs[1][rows, :] = jnp.broadcast_to(high, (ROWS, DH))
            outs[2][rows, :] = jnp.broadcast_to(total, (ROWS, DH))


def flash(first, last, queries, pieces, state):
    n = len(pieces)
    keys = n * pieces[0].shape[0]
    nq = HEADS * ROWS
    if last:
        shapes = [jax.ShapeDtypeStruct((ROWS, DH), BF)] * HEADS
    else:
        shapes = [jax.ShapeDtypeStruct((nq, DH), F32)] * 3
    return pl.pallas_call(
        functools.partial(flash_kernel, first, last, n, 1152),
        out_shape=shapes,
        in_specs=[VM] * HEADS + [ANY] * n + [VM] * len(state),
        out_specs=[VM] * len(shapes),
        scratch_shapes=[pltpu.VMEM((keys, 2 * DH), BF), pltpu.SemaphoreType.DMA((n,))],
        compiler_params=pltpu.CompilerParams(vmem_limit_bytes=VLIM),
        cost_estimate=pl.CostEstimate(flops=1000, bytes_accessed=1000, transcendentals=0),
    )(*queries, *pieces, *state)


def project_kernel(steps, first, last, pos_ref, w_hbm, *refs):
    n = len(steps)
    blocks, refs = refs[:n], refs[n:]
    if not first:
        acc_ref, refs = refs[0], refs[1:]
    outs, (weight, tokens, sems) = refs[: 1 + last], refs[1 + last :]
    turn, col, core = pos_ref[0], pos_ref[1], pos_ref[2]
    wide = HEADS * DH
    copies = []
    for k, s in enumerate(steps):
        source = lax.rem(col + NY - s, NY)
        rows = pl.ds(pl.multiple_of(source * wide, wide), wide)
        copies.append(pltpu.make_async_copy(w_hbm.at[rows], weight.at[k], sems.at[k]))
    for c in copies:
        c.start()
    for k in range(n):
        for j in range(HEADS):
            head = lax.rem(turn + j, HEADS)
            cols = pl.ds(pl.multiple_of(head * DH, DH), DH)
            for i in range(2):
                rows = pl.ds(pl.multiple_of(lax.rem(core + i, 2) * HALF, 16), HALF)
                tokens[k, i * HALF : (i + 1) * HALF, cols] = blocks[k][rows, j * DH : (j + 1) * DH]
    for c in copies:
        c.wait()
    total = None if first else acc_ref[...]
    for k in range(n):
        part = jnp.dot(tokens[k], weight[k], preferred_element_type=F32)
        total = part if total is None else total + part
    if last:
        outs[0][...] = total[:HALF]
        outs[1][...] = total[HALF:].astype(BF)
    else:
        outs[0][...] = total


def project(steps, last, pos, weight, blocks, *total):
    n = len(steps)
    wide, width = HEADS * DH, weight.shape[1]
    if last:
        shapes = [jax.ShapeDtypeStruct((HALF, width), t) for t in (F32, BF)]
    else:
        shapes = [jax.ShapeDtypeStruct((ROWS, width), F32)]
    return pl.pallas_call(
        functools.partial(project_kernel, steps, not total, last),
        out_shape=shapes,
        in_specs=[SM, ANY] + [VM] * (n + len(total)),
        out_specs=[VM] * len(shapes),
        scratch_shapes=[
            pltpu.VMEM((n, wide, width), BF),
            pltpu.VMEM((n, ROWS, wide), BF),
            pltpu.SemaphoreType.DMA((n,)),
        ],
        compiler_params=pltpu.CompilerParams(vmem_limit_bytes=VLIM),
    )(pos, weight, *blocks, *total)


def owner_pairs(j):
    return [
        (z * NC + c, (HEADS * c + (z + j) % HEADS) * NC + z // HEADS)
        for z in range(NZ)
        for c in range(NC)
    ]


def to_owner(value, j):
    return lax.ppermute(value, ("z", "row"), owner_pairs(j))


def from_owner(value, j):
    return lax.ppermute(value, ("z", "row"), [(b, a) for a, b in owner_pairs(j)])


def shift(value, axis, size, step):
    if step == 0:
        return value
    return lax.ppermute(value, axis, [(i, (i + step) % size) for i in range(size)])


def swap(value):
    return lax.ppermute(value, "row", [(0, 1), (1, 0)])


def body(query_proj, key_proj, value_proj, query_gain, key_gain, residual, out_weight):
    pos = jnp.stack([lax.axis_index(a) for a in ("z", "col", "row")]).astype(jnp.int32)
    ready = norms(
        pos, key_proj, key_gain.reshape(1, -1), value_proj, query_proj, query_gain.reshape(1, -1)
    )
    held = [to_owner(ready[j], j) for j in range(HEADS)]
    own = jnp.concatenate([m[:, : 2 * DH] for m in held], axis=0)
    near, back = shift(own, "x", NX, 1), shift(own, "x", NX, -1)
    state = flash(True, False, held, [own, swap(own)], ())
    half = own.shape[0] // 2
    far = [shift(near[:half], "x", NX, 1), shift(back[half:], "x", NX, -1)]
    near, back, *state = lax.optimization_barrier((near, back, *state))
    state = flash(False, False, held, [near, back, swap(near), swap(back)], state)
    *far, a, b, c = lax.optimization_barrier((*far, *state))
    attended = flash(False, True, held, far + [swap(p) for p in far], (a, b, c))
    mine = jnp.concatenate([from_owner(attended[j], j) for j in range(HEADS)], axis=1)
    far, near, back = [shift(mine, "col", NY, s) for s in (2, 1, 3)]
    total = project((0,), False, pos, out_weight, [mine])
    near, back, *total = lax.optimization_barrier((near, back, *total))
    total = project((1, 3), False, pos, out_weight, [near, back], *total)
    far, *total = lax.optimization_barrier((far, *total))
    keep, send = project((2,), True, pos, out_weight, [far], *total)
    return (residual.astype(F32) + (keep + swap(send).astype(F32))).astype(BF)


def solution(mesh):
    fine = Mesh(mesh.devices.reshape(NZ, NX, NC, NY), ("z", "x", "row", "col"))
    seq = ("z", "x")
    heads = ("row", "col")
    placed = (
        P(seq, heads),
        P(seq, heads),
        P(seq, heads),
        P(heads),
        P(heads),
        P(("z", "x", "row"), "col"),
        P("row", "col"),
    )
    return jax.shard_map(
        body, mesh=fine, in_specs=placed, out_specs=P(("z", "x", "row"), "col"), check_vma=False
    )
```

```python
import functools
import math

import jax
import jax.numpy as jnp
from jax import lax
from jax.experimental import pallas as pl
from jax.experimental.pallas import tpu as pltpu
from jax.sharding import Mesh, PartitionSpec as P

DH = 128
EPS = 1e-06
BF = jnp.bfloat16
F32 = jnp.float32
NZ, NX, NC, NY = 8, 4, 2, 4
ROWS = 288
HALF = ROWS // 2
HEADS = 4
SENDS = (3, 1, 2, 0)
NT = (((1,), (1,)), ((), ()))
VM = pl.BlockSpec(memory_space=pltpu.VMEM)
SM = pl.BlockSpec(memory_space=pltpu.MemorySpace.SMEM)
ANY = pl.BlockSpec(memory_space=pl.ANY)
VLIM = 40 << 20


def norm(values, gain):
    centre = jnp.mean(values, axis=-1, keepdims=True)
    shifted = values - centre
    variance = jnp.mean(shifted * shifted, axis=-1, keepdims=True)
    return shifted * lax.rsqrt(variance + EPS) * gain


def norm_kernel(pos_ref, *refs):
    sources, outs, held, sems = refs[:5], refs[5:9], refs[9:14], refs[14]
    copies = [
        pltpu.make_async_copy(a, b, sems.at[i]) for i, (a, b) in enumerate(zip(sources, held))
    ]
    for c in copies:
        c.start()
    k_ref, kg_ref, v_ref, q_ref, qg_ref = held
    heads = [lax.rem(pos_ref[0] + j, HEADS) for j in SENDS]
    columns = [pl.ds(pl.multiple_of(h * DH, DH), DH) for h in heads]
    copies[0].wait()
    copies[1].wait()
    for out, cols in zip(outs, columns):
        out[:, :DH] = norm(k_ref[:, cols].astype(F32), kg_ref[:, cols]).astype(BF)
    copies[2].wait()
    for out, cols in zip(outs, columns):
        out[:, DH : 2 * DH] = v_ref[:, cols]
    copies[3].wait()
    copies[4].wait()
    for out, cols in zip(outs, columns):
        queries = norm(q_ref[:, cols].astype(F32), qg_ref[:, cols])
        out[:, 2 * DH :] = (queries * (1.0 / math.sqrt(DH))).astype(BF)


def norms(pos, *arrays):
    return pl.pallas_call(
        norm_kernel,
        out_shape=[jax.ShapeDtypeStruct((ROWS, 3 * DH), BF)] * HEADS,
        in_specs=[SM] + [ANY] * 5,
        out_specs=[VM] * HEADS,
        scratch_shapes=[pltpu.VMEM(a.shape, a.dtype) for a in arrays]
        + [pltpu.SemaphoreType.DMA((5,))],
        compiler_params=pltpu.CompilerParams(vmem_limit_bytes=62 << 20),
    )(pos, *arrays)


def flash_kernel(first, last, nq, nkv, most, *refs):
    queries, refs = refs[:nq], refs[nq:]
    pieces, refs = refs[:nkv], refs[nkv:]
    if not first:
        (acc_in, max_in, sum_in), refs = refs[:3], refs[3:]
    outs = refs
    blocks, size = [[]], 0
    for p in pieces:
        if size + p.shape[0] > most and blocks[-1]:
            blocks.append([])
            size = 0
        blocks[-1].append(p)
        size += p.shape[0]
    for i in range(nq):
        rows = slice(i * ROWS, (i + 1) * ROWS)
        q = queries[i][:, 2 * DH :]

        def scores(block):
            parts = [
                lax.dot_general(q, p[:, :DH], NT, preferred_element_type=F32) for p in block
            ]
            return jnp.concatenate(parts, axis=1)

        if first:
            high = None
        else:
            high, total, acc = max_in[rows, :1], sum_in[rows, :1], acc_in[rows, :]
        ahead = scores(blocks[0])
        for b, block in enumerate(blocks):
            s = ahead
            if b + 1 < len(blocks):
                ahead = scores(blocks[b + 1])
            top = jnp.max(s, axis=1, keepdims=True)
            top = top if high is None else jnp.maximum(high, top)
            weights = jnp.exp(s - top).astype(BF)
            values = jnp.concatenate([p[:, DH : 2 * DH] for p in block], axis=0)
            both = jnp.dot(
                weights,
                jnp.concatenate([values, jnp.ones_like(values)], axis=1),
                preferred_element_type=F32,
            )
            part, psum = both[:, :DH], both[:, DH : DH + 1]
            if high is None:
                acc, total = part, psum
            else:
                scale = jnp.exp(high - top)
                acc, total = acc * scale + part, total * scale + psum
            high = top
        if last:
            outs[i][...] = (acc / total).astype(BF)
        else:
            outs[0][rows, :] = acc
            outs[1][rows, :] = jnp.broadcast_to(high, (ROWS, DH))
            outs[2][rows, :] = jnp.broadcast_to(total, (ROWS, DH))


def flash(last, queries, pieces, state=(), most=2304):
    n, nq = len(pieces), len(queries)
    if last:
        shapes = [jax.ShapeDtypeStruct((ROWS, DH), BF)] * nq
    else:
        shapes = [jax.ShapeDtypeStruct((nq * ROWS, DH), F32)] * 3
    return pl.pallas_call(
        functools.partial(flash_kernel, not state, last, nq, n, most),
        out_shape=shapes,
        in_specs=[VM] * (nq + n + len(state)),
        out_specs=[VM] * len(shapes),
        compiler_params=pltpu.CompilerParams(vmem_limit_bytes=VLIM),
        cost_estimate=pl.CostEstimate(flops=1000, bytes_accessed=1000, transcendentals=0),
    )(*queries, *pieces, *state)


def project_kernel(steps, first, last, pos_ref, w_hbm, *refs):
    n = len(steps)
    blocks, refs = refs[:n], refs[n:]
    if not first:
        acc_ref, refs = refs[0], refs[1:]
    outs, (weight, tokens, sems) = refs[: 1 + last], refs[1 + last :]
    turn, col, core = pos_ref[0], pos_ref[1], pos_ref[2]
    wide = HEADS * DH
    copies = []
    for k, s in enumerate(steps):
        source = lax.rem(col + NY - s, NY)
        rows = pl.ds(pl.multiple_of(source * wide, wide), wide)
        copies.append(pltpu.make_async_copy(w_hbm.at[rows], weight.at[k], sems.at[k]))
    for c in copies:
        c.start()
    for k in range(n):
        for j in range(HEADS):
            head = lax.rem(turn + SENDS[j], HEADS)
            cols = pl.ds(pl.multiple_of(head * DH, DH), DH)
            for i in range(2):
                rows = pl.ds(pl.multiple_of(lax.rem(core + i, 2) * HALF, 16), HALF)
                tokens[k, i * HALF : (i + 1) * HALF, cols] = blocks[k][rows, j * DH : (j + 1) * DH]
    for c in copies:
        c.wait()
    total = None if first else acc_ref[...]
    for k in range(n):
        part = jnp.dot(tokens[k], weight[k], preferred_element_type=F32)
        total = part if total is None else total + part
    if last:
        outs[0][...] = total[:HALF]
        outs[1][...] = total[HALF:].astype(BF)
    else:
        outs[0][...] = total


def project(steps, last, pos, weight, blocks, *total):
    n = len(steps)
    wide, width = HEADS * DH, weight.shape[1]
    if last:
        shapes = [jax.ShapeDtypeStruct((HALF, width), t) for t in (F32, BF)]
    else:
        shapes = [jax.ShapeDtypeStruct((ROWS, width), F32)]
    return pl.pallas_call(
        functools.partial(project_kernel, steps, not total, last),
        out_shape=shapes,
        in_specs=[SM, ANY] + [VM] * (n + len(total)),
        out_specs=[VM] * len(shapes),
        scratch_shapes=[
            pltpu.VMEM((n, wide, width), BF),
            pltpu.VMEM((n, ROWS, wide), BF),
            pltpu.SemaphoreType.DMA((n,)),
        ],
        compiler_params=pltpu.CompilerParams(vmem_limit_bytes=VLIM),
    )(pos, weight, *blocks, *total)


def owner_pairs(j):
    return [
        (z * NC + c, (HEADS * c + (z + SENDS[j]) % HEADS) * NC + z // HEADS)
        for z in range(NZ)
        for c in range(NC)
    ]


def to_owner(value, j):
    return lax.ppermute(value, ("z", "row"), owner_pairs(j))


def from_owner(value, j):
    return lax.ppermute(value, ("z", "row"), [(b, a) for a, b in owner_pairs(j)])


def shift(value, axis, size, step):
    if step == 0:
        return value
    return lax.ppermute(value, axis, [(i, (i + step) % size) for i in range(size)])


def swap(value):
    return lax.ppermute(value, "row", [(0, 1), (1, 0)])


def body(query_proj, key_proj, value_proj, query_gain, key_gain, residual, out_weight):
    pos = jnp.stack([lax.axis_index(a) for a in ("z", "col", "row")]).astype(jnp.int32)
    ready = norms(
        pos, key_proj, key_gain.reshape(1, -1), value_proj, query_proj, query_gain.reshape(1, -1)
    )
    held = [to_owner(ready[j], j) for j in range(HEADS)]
    own = jnp.concatenate([m[:, : 2 * DH] for m in held], axis=0)
    near, back = shift(own, "x", NX, 1), shift(own, "x", NX, -1)
    state = flash(False, held, [own])
    half = own.shape[0] // 2
    far = [shift(near[:half], "x", NX, 1), shift(back[half:], "x", NX, -1)]
    near, back, *state = lax.optimization_barrier((near, back, *state))
    state = flash(False, held, [swap(own), near, back, swap(near), swap(back)], state)
    *far, a, b, c = lax.optimization_barrier((*far, *state))
    attended = flash(True, held, far + [swap(p) for p in far], (a, b, c))
    mine = jnp.concatenate([from_owner(attended[j], j) for j in range(HEADS)], axis=1)
    far, near, back = [shift(mine, "col", NY, s) for s in (2, 1, 3)]
    total = project((0,), False, pos, out_weight, [mine])
    near, back, *total = lax.optimization_barrier((near, back, *total))
    total = project((1, 3), False, pos, out_weight, [near, back], *total)
    far, *total = lax.optimization_barrier((far, *total))
    keep, send = project((2,), True, pos, out_weight, [far], *total)
    return (residual.astype(F32) + (keep + swap(send).astype(F32))).astype(BF)


def solution(mesh):
    fine = Mesh(mesh.devices.reshape(NZ, NX, NC, NY), ("z", "x", "row", "col"))
    seq = ("z", "x")
    heads = ("row", "col")
    placed = (
        P(seq, heads),
        P(seq, heads),
        P(seq, heads),
        P(heads),
        P(heads),
        P(("z", "x", "row"), "col"),
        P("row", "col"),
    )
    return jax.shard_map(
        body, mesh=fine, in_specs=placed, out_specs=P(("z", "x", "row"), "col"), check_vma=False
    )
```

```python
import functools
import math

import jax
import jax.numpy as jnp
from jax import lax
from jax.experimental import pallas as pl
from jax.experimental.pallas import tpu as pltpu
from jax.sharding import Mesh, PartitionSpec as P

DH = 128
EPS = 1e-06
BF = jnp.bfloat16
F32 = jnp.float32
NZ, NX, NC, NY = 8, 4, 2, 4
ROWS = 288
HALF = ROWS // 2
HEADS = 4
SENDS = (3, 2, 1, 0)
NT = (((1,), (1,)), ((), ()))
VM = pl.BlockSpec(memory_space=pltpu.VMEM)
ANY = pl.BlockSpec(memory_space=pl.ANY)
VLIM = 40 << 20


def norm(values, gain):
    centre = jnp.mean(values, axis=-1, keepdims=True)
    shifted = values - centre
    variance = jnp.mean(shifted * shifted, axis=-1, keepdims=True)
    return shifted * lax.rsqrt(variance + EPS) * gain


def norm_kernel(*refs):
    sources, outs, held, sems = refs[:5], refs[5:9], refs[9:14], refs[14]
    copies = [
        pltpu.make_async_copy(a, b, sems.at[i]) for i, (a, b) in enumerate(zip(sources, held))
    ]
    for c in copies:
        c.start()
    k_ref, kg_ref, v_ref, q_ref, qg_ref = held
    turn = lax.axis_index("z")
    heads = [lax.rem(turn + j, HEADS) for j in SENDS]
    columns = [pl.ds(pl.multiple_of(h * DH, DH), DH) for h in heads]
    copies[0].wait()
    copies[1].wait()
    for out, cols in zip(outs, columns):
        out[:, :DH] = norm(k_ref[:, cols].astype(F32), kg_ref[:, cols]).astype(BF)
    copies[2].wait()
    for out, cols in zip(outs, columns):
        out[:, DH : 2 * DH] = v_ref[:, cols]
    copies[3].wait()
    copies[4].wait()
    for out, cols in zip(outs, columns):
        queries = norm(q_ref[:, cols].astype(F32), qg_ref[:, cols])
        out[:, 2 * DH :] = (queries * (1.0 / math.sqrt(DH))).astype(BF)


def norms(*arrays):
    return pl.pallas_call(
        norm_kernel,
        out_shape=[jax.ShapeDtypeStruct((ROWS, 3 * DH), BF)] * HEADS,
        in_specs=[ANY] * 5,
        out_specs=[VM] * HEADS,
        scratch_shapes=[pltpu.VMEM(a.shape, a.dtype) for a in arrays]
        + [pltpu.SemaphoreType.DMA((5,))],
        compiler_params=pltpu.CompilerParams(vmem_limit_bytes=62 << 20),
    )(*arrays)


def flash_kernel(first, last, nq, nkv, most, *refs):
    queries, refs = refs[:nq], refs[nq:]
    pieces, refs = refs[:nkv], refs[nkv:]
    if not first:
        (acc_in, max_in, sum_in), refs = refs[:3], refs[3:]
    outs = refs
    blocks, size = [[]], 0
    for p in pieces:
        if size + p.shape[0] > most and blocks[-1]:
            blocks.append([])
            size = 0
        blocks[-1].append(p)
        size += p.shape[0]
    for i in range(nq):
        rows = slice(i * ROWS, (i + 1) * ROWS)
        q = queries[i][:, 2 * DH :]

        def scores(block):
            keys = jnp.concatenate([p[:, :DH] for p in block], axis=0)
            return lax.dot_general(q, keys, NT, preferred_element_type=F32)

        if first:
            high = None
        else:
            high, total, acc = max_in[rows, :1], sum_in[rows, :1], acc_in[rows, :]
        ahead = scores(blocks[0])
        for b, block in enumerate(blocks):
            s = ahead
            if b + 1 < len(blocks):
                ahead = scores(blocks[b + 1])
            top = jnp.max(s, axis=1, keepdims=True)
            top = top if high is None else jnp.maximum(high, top)
            weights = jnp.exp(s - top).astype(BF)
            values = jnp.concatenate([p[:, DH : 2 * DH] for p in block], axis=0)
            both = jnp.dot(
                weights,
                jnp.concatenate([values, jnp.ones_like(values)], axis=1),
                preferred_element_type=F32,
            )
            part, psum = both[:, :DH], both[:, DH : DH + 1]
            if high is None:
                acc, total = part, psum
            else:
                scale = jnp.exp(high - top)
                acc, total = acc * scale + part, total * scale + psum
            high = top
        if last:
            outs[i][...] = (acc / total).astype(BF)
        else:
            outs[0][rows, :] = acc
            outs[1][rows, :] = jnp.broadcast_to(high, (ROWS, DH))
            outs[2][rows, :] = jnp.broadcast_to(total, (ROWS, DH))


def flash(last, queries, pieces, state=(), most=2304):
    n, nq = len(pieces), len(queries)
    if last:
        shapes = [jax.ShapeDtypeStruct((ROWS, DH), BF)] * nq
    else:
        shapes = [jax.ShapeDtypeStruct((nq * ROWS, DH), F32)] * 3
    return pl.pallas_call(
        functools.partial(flash_kernel, not state, last, nq, n, most),
        out_shape=shapes,
        in_specs=[VM] * (nq + n + len(state)),
        out_specs=[VM] * len(shapes),
        compiler_params=pltpu.CompilerParams(vmem_limit_bytes=VLIM),
        cost_estimate=pl.CostEstimate(flops=1000, bytes_accessed=1000, transcendentals=0),
    )(*queries, *pieces, *state)


def project_kernel(steps, first, last, w_hbm, *refs):
    n = len(steps)
    blocks, refs = refs[:n], refs[n:]
    if not first:
        acc_ref, refs = refs[0], refs[1:]
    outs, (weight, tokens, sems) = refs[: 1 + last], refs[1 + last :]
    turn, col, core = [lax.axis_index(a) for a in ("z", "col", "row")]
    wide = HEADS * DH
    copies = []
    for k, s in enumerate(steps):
        source = lax.rem(col + NY - s, NY)
        rows = pl.ds(pl.multiple_of(source * wide, wide), wide)
        copies.append(pltpu.make_async_copy(w_hbm.at[rows], weight.at[k], sems.at[k]))
    for c in copies:
        c.start()
    for k in range(n):
        for j in range(HEADS):
            head = lax.rem(turn + SENDS[j], HEADS)
            cols = pl.ds(pl.multiple_of(head * DH, DH), DH)
            for i in range(2):
                rows = pl.ds(pl.multiple_of(lax.rem(core + i, 2) * HALF, 16), HALF)
                tokens[k, i * HALF : (i + 1) * HALF, cols] = blocks[k][rows, j * DH : (j + 1) * DH]
    for c in copies:
        c.wait()
    total = None if first else acc_ref[...]
    for k in range(n):
        part = jnp.dot(tokens[k], weight[k], preferred_element_type=F32)
        total = part if total is None else total + part
    if last:
        outs[0][...] = total[:HALF]
        outs[1][...] = total[HALF:].astype(BF)
    else:
        outs[0][...] = total


def project(steps, last, weight, blocks, *total):
    n = len(steps)
    wide, width = HEADS * DH, weight.shape[1]
    if last:
        shapes = [jax.ShapeDtypeStruct((HALF, width), t) for t in (F32, BF)]
    else:
        shapes = [jax.ShapeDtypeStruct((ROWS, width), F32)]
    return pl.pallas_call(
        functools.partial(project_kernel, steps, not total, last),
        out_shape=shapes,
        in_specs=[ANY] + [VM] * (n + len(total)),
        out_specs=[VM] * len(shapes),
        scratch_shapes=[
            pltpu.VMEM((n, wide, width), BF),
            pltpu.VMEM((n, ROWS, wide), BF),
            pltpu.SemaphoreType.DMA((n,)),
        ],
        compiler_params=pltpu.CompilerParams(vmem_limit_bytes=VLIM),
    )(weight, *blocks, *total)


def owner_pairs(j):
    return [
        (z * NC + c, (HEADS * c + (z + SENDS[j]) % HEADS) * NC + z // HEADS)
        for z in range(NZ)
        for c in range(NC)
    ]


def to_owner(value, j):
    return lax.ppermute(value, ("z", "row"), owner_pairs(j))


def from_owner(value, j):
    return lax.ppermute(value, ("z", "row"), [(b, a) for a, b in owner_pairs(j)])


def shift(value, axis, size, step):
    if step == 0:
        return value
    return lax.ppermute(value, axis, [(i, (i + step) % size) for i in range(size)])


def swap(value):
    return lax.ppermute(value, "row", [(0, 1), (1, 0)])


def body(query_proj, key_proj, value_proj, query_gain, key_gain, residual, out_weight):
    ready = norms(
        key_proj, key_gain.reshape(1, -1), value_proj, query_proj, query_gain.reshape(1, -1)
    )
    held = [to_owner(ready[j], j) for j in range(HEADS)]
    own = jnp.concatenate([m[:, : 2 * DH] for m in held], axis=0)
    near, back = shift(own, "x", NX, 1), shift(own, "x", NX, -1)
    state = flash(False, held, [own])
    half = own.shape[0] // 2
    far = [shift(near[:half], "x", NX, 1), shift(back[half:], "x", NX, -1)]
    near, back, *state = lax.optimization_barrier((near, back, *state))
    state = flash(False, held, [swap(own), near, back, swap(near), swap(back)], state)
    *far, a, b, c = lax.optimization_barrier((*far, *state))
    attended = flash(True, held, far + [swap(p) for p in far], (a, b, c))
    mine = jnp.concatenate([from_owner(attended[j], j) for j in range(HEADS)], axis=1)
    far, near, back = [shift(mine, "col", NY, s) for s in (2, 1, 3)]
    total = project((0,), False, out_weight, [mine])
    near, back, *total = lax.optimization_barrier((near, back, *total))
    total = project((1, 3), False, out_weight, [near, back], *total)
    far, *total = lax.optimization_barrier((far, *total))
    keep, send = project((2,), True, out_weight, [far], *total)
    return (residual.astype(F32) + (keep + swap(send).astype(F32))).astype(BF)


def solution(mesh):
    fine = Mesh(mesh.devices.reshape(NZ, NX, NC, NY), ("z", "x", "row", "col"))
    seq = ("z", "x")
    heads = ("row", "col")
    placed = (
        P(seq, heads),
        P(seq, heads),
        P(seq, heads),
        P(heads),
        P(heads),
        P(("z", "x", "row"), "col"),
        P("row", "col"),
    )
    return jax.shard_map(
        body, mesh=fine, in_specs=placed, out_specs=P(("z", "x", "row"), "col"), check_vma=False
    )
```

```python
import functools
import math

import jax
import jax.numpy as jnp
from jax import lax
from jax.experimental import pallas as pl
from jax.experimental.pallas import tpu as pltpu
from jax.sharding import Mesh, PartitionSpec as P

DH = 128
EPS = 1e-06
BF = jnp.bfloat16
F32 = jnp.float32
NZ, NX, NC, NY = 8, 4, 2, 4
ROWS = 288
HALF = ROWS // 2
HEADS = 4
SENDS = (3, 2, 1, 0)
NT = (((1,), (1,)), ((), ()))
VM = pl.BlockSpec(memory_space=pltpu.VMEM)
ANY = pl.BlockSpec(memory_space=pl.ANY)
VLIM = 40 << 20


def norm(values, gain):
    centre = jnp.mean(values, axis=-1, keepdims=True)
    shifted = values - centre
    variance = jnp.mean(shifted * shifted, axis=-1, keepdims=True)
    return shifted * lax.rsqrt(variance + EPS) * gain


def norm_kernel(*refs):
    sources, outs, held, sems = refs[:5], refs[5:9], refs[9:14], refs[14]
    copies = [
        pltpu.make_async_copy(a, b, sems.at[i]) for i, (a, b) in enumerate(zip(sources, held))
    ]
    for c in copies:
        c.start()
    k_ref, kg_ref, v_ref, q_ref, qg_ref = held
    turn = lax.axis_index("z")
    heads = [lax.rem(turn + j, HEADS) for j in SENDS]
    columns = [pl.ds(pl.multiple_of(h * DH, DH), DH) for h in heads]
    copies[0].wait()
    copies[1].wait()
    for out, cols in zip(outs, columns):
        out[:, :DH] = norm(k_ref[:, cols].astype(F32), kg_ref[:, cols]).astype(BF)
    copies[2].wait()
    for out, cols in zip(outs, columns):
        out[:, DH : 2 * DH] = v_ref[:, cols]
    copies[3].wait()
    copies[4].wait()
    for out, cols in zip(outs, columns):
        queries = norm(q_ref[:, cols].astype(F32), qg_ref[:, cols])
        out[:, 2 * DH :] = (queries * (1.0 / math.sqrt(DH))).astype(BF)


def norms(*arrays):
    return pl.pallas_call(
        norm_kernel,
        out_shape=[jax.ShapeDtypeStruct((ROWS, 3 * DH), BF)] * HEADS,
        in_specs=[ANY] * 5,
        out_specs=[VM] * HEADS,
        scratch_shapes=[pltpu.VMEM(a.shape, a.dtype) for a in arrays]
        + [pltpu.SemaphoreType.DMA((5,))],
        compiler_params=pltpu.CompilerParams(vmem_limit_bytes=62 << 20),
    )(*arrays)


def flash_kernel(first, last, nq, nkv, most, *refs):
    queries, refs = refs[:nq], refs[nq:]
    pieces, refs = refs[:nkv], refs[nkv:]
    if not first:
        (acc_in, max_in, sum_in), refs = refs[:3], refs[3:]
    outs = refs
    blocks, size = [[]], 0
    for p in pieces:
        if size + p.shape[0] > most and blocks[-1]:
            blocks.append([])
            size = 0
        blocks[-1].append(p)
        size += p.shape[0]
    for i in range(nq):
        rows = slice(i * ROWS, (i + 1) * ROWS)
        q = queries[i][:, 2 * DH :]

        def scores(block):
            keys = jnp.concatenate([p[:, :DH] for p in block], axis=0)
            return lax.dot_general(q, keys, NT, preferred_element_type=F32)

        if first:
            high = None
        else:
            high, total, acc = max_in[rows, :1], sum_in[rows, :1], acc_in[rows, :]
        ahead = scores(blocks[0])
        for b, block in enumerate(blocks):
            s = ahead
            if b + 1 < len(blocks):
                ahead = scores(blocks[b + 1])
            top = jnp.max(s, axis=1, keepdims=True)
            top = top if high is None else jnp.maximum(high, top)
            weights = jnp.exp(s - top).astype(BF)
            values = jnp.concatenate([p[:, DH : 2 * DH] for p in block], axis=0)
            both = jnp.dot(
                weights,
                jnp.concatenate([values, jnp.ones_like(values)], axis=1),
                preferred_element_type=F32,
            )
            part, psum = both[:, :DH], both[:, DH : DH + 1]
            if high is None:
                acc, total = part, psum
            else:
                scale = jnp.exp(high - top)
                acc, total = acc * scale + part, total * scale + psum
            high = top
        if last:
            outs[i][...] = (acc / total).astype(BF)
        else:
            outs[0][rows, :] = acc
            outs[1][rows, :] = jnp.broadcast_to(high, (ROWS, DH))
            outs[2][rows, :] = jnp.broadcast_to(total, (ROWS, DH))


def flash(last, queries, pieces, state=(), most=2304):
    n, nq = len(pieces), len(queries)
    if last:
        shapes = [jax.ShapeDtypeStruct((ROWS, DH), BF)] * nq
    else:
        shapes = [jax.ShapeDtypeStruct((nq * ROWS, DH), F32)] * 3
    return pl.pallas_call(
        functools.partial(flash_kernel, not state, last, nq, n, most),
        out_shape=shapes,
        in_specs=[VM] * (nq + n + len(state)),
        out_specs=[VM] * len(shapes),
        compiler_params=pltpu.CompilerParams(vmem_limit_bytes=VLIM),
        cost_estimate=pl.CostEstimate(flops=1000, bytes_accessed=1000, transcendentals=0),
    )(*queries, *pieces, *state)


def project_kernel(steps, first, last, w_hbm, *refs):
    n = len(steps)
    blocks, refs = refs[:n], refs[n:]
    if not first:
        acc_ref, refs = refs[0], refs[1:]
    outs, (weight, tokens, sems) = refs[: 1 + last], refs[1 + last :]
    turn, col, core = [lax.axis_index(a) for a in ("z", "col", "row")]
    wide = HEADS * DH
    copies = []
    for k, s in enumerate(steps):
        source = lax.rem(col + NY - s, NY)
        rows = pl.ds(pl.multiple_of(source * wide, wide), wide)
        copies.append(pltpu.make_async_copy(w_hbm.at[rows], weight.at[k], sems.at[k]))
    for c in copies:
        c.start()
    for k in range(n):
        for j in range(HEADS):
            head = lax.rem(turn + SENDS[j], HEADS)
            cols = pl.ds(pl.multiple_of(head * DH, DH), DH)
            for i in range(2):
                rows = pl.ds(pl.multiple_of(lax.rem(core + i, 2) * HALF, 16), HALF)
                tokens[k, i * HALF : (i + 1) * HALF, cols] = blocks[k][rows, j * DH : (j + 1) * DH]
    for c in copies:
        c.wait()
    total = None if first else acc_ref[...]
    for k in range(n):
        part = jnp.dot(tokens[k], weight[k], preferred_element_type=F32)
        total = part if total is None else total + part
    if last:
        outs[0][...] = total[:HALF]
        outs[1][...] = total[HALF:].astype(BF)
    else:
        outs[0][...] = total


def project(steps, last, weight, blocks, *total):
    n = len(steps)
    wide, width = HEADS * DH, weight.shape[1]
    if last:
        shapes = [jax.ShapeDtypeStruct((HALF, width), t) for t in (F32, BF)]
    else:
        shapes = [jax.ShapeDtypeStruct((ROWS, width), F32)]
    return pl.pallas_call(
        functools.partial(project_kernel, steps, not total, last),
        out_shape=shapes,
        in_specs=[ANY] + [VM] * (n + len(total)),
        out_specs=[VM] * len(shapes),
        scratch_shapes=[
            pltpu.VMEM((n, wide, width), BF),
            pltpu.VMEM((n, ROWS, wide), BF),
            pltpu.SemaphoreType.DMA((n,)),
        ],
        compiler_params=pltpu.CompilerParams(vmem_limit_bytes=VLIM),
    )(weight, *blocks, *total)


def owner_pairs(j):
    return [
        (z * NC + c, (HEADS * c + (z + SENDS[j]) % HEADS) * NC + z // HEADS)
        for z in range(NZ)
        for c in range(NC)
    ]


def to_owner(value, j):
    return lax.ppermute(value, ("z", "row"), owner_pairs(j))


def from_owner(value, j):
    return lax.ppermute(value, ("z", "row"), [(b, a) for a, b in owner_pairs(j)])


def shift(value, axis, size, step):
    if step == 0:
        return value
    return lax.ppermute(value, axis, [(i, (i + step) % size) for i in range(size)])


def swap(value):
    return lax.ppermute(value, "row", [(0, 1), (1, 0)])


def body(query_proj, key_proj, value_proj, query_gain, key_gain, residual, out_weight):
    ready = norms(
        key_proj, key_gain.reshape(1, -1), value_proj, query_proj, query_gain.reshape(1, -1)
    )
    held = [to_owner(ready[j], j) for j in range(HEADS)]
    own = jnp.concatenate([m[:, : 2 * DH] for m in held], axis=0)
    near, back = shift(own, "x", NX, 1), shift(own, "x", NX, -1)
    half = own.shape[0] // 2
    state = flash(False, held, [own, swap(own[:half]), swap(own[half:])])
    half = own.shape[0] // 2
    far = [shift(near[:half], "x", NX, 1), shift(back[half:], "x", NX, -1)]
    near, back, *state = lax.optimization_barrier((near, back, *state))
    state = flash(False, held, [near, back, swap(near), swap(back)], state)
    *far, a, b, c = lax.optimization_barrier((*far, *state))
    attended = flash(True, held, far + [swap(p) for p in far], (a, b, c))
    mine = jnp.concatenate([from_owner(attended[j], j) for j in range(HEADS)], axis=1)
    far, near, back = [shift(mine, "col", NY, s) for s in (2, 1, 3)]
    total = project((0,), False, out_weight, [mine])
    near, back, *total = lax.optimization_barrier((near, back, *total))
    total = project((1, 3), False, out_weight, [near, back], *total)
    far, *total = lax.optimization_barrier((far, *total))
    keep, send = project((2,), True, out_weight, [far], *total)
    return (residual.astype(F32) + (keep + swap(send).astype(F32))).astype(BF)


def solution(mesh):
    fine = Mesh(mesh.devices.reshape(NZ, NX, NC, NY), ("z", "x", "row", "col"))
    seq = ("z", "x")
    heads = ("row", "col")
    placed = (
        P(seq, heads),
        P(seq, heads),
        P(seq, heads),
        P(heads),
        P(heads),
        P(("z", "x", "row"), "col"),
        P("row", "col"),
    )
    return jax.shard_map(
        body, mesh=fine, in_specs=placed, out_specs=P(("z", "x", "row"), "col"), check_vma=False
    )
```

```python
import functools
import math

import jax
import jax.numpy as jnp
from jax import lax
from jax.experimental import pallas as pl
from jax.experimental.pallas import tpu as pltpu
from jax.sharding import Mesh, PartitionSpec as P

DH = 128
EPS = 1e-06
BF = jnp.bfloat16
F32 = jnp.float32
NZ, NX, NC, NY = 8, 4, 2, 4
ROWS = 288
HALF = ROWS // 2
HEADS = 4
SENDS = (3, 2, 1, 0)
NT = (((1,), (1,)), ((), ()))
VM = pl.BlockSpec(memory_space=pltpu.VMEM)
ANY = pl.BlockSpec(memory_space=pl.ANY)
VLIM = 40 << 20


def norm(values, gain):
    centre = jnp.mean(values, axis=-1, keepdims=True)
    shifted = values - centre
    variance = jnp.mean(shifted * shifted, axis=-1, keepdims=True)
    return shifted * lax.rsqrt(variance + EPS) * gain


def norm_kernel(*refs):
    sources, outs, held, sems = refs[:5], refs[5:9], refs[9:14], refs[14]
    copies = [
        pltpu.make_async_copy(a, b, sems.at[i]) for i, (a, b) in enumerate(zip(sources, held))
    ]
    for c in copies:
        c.start()
    k_ref, kg_ref, v_ref, q_ref, qg_ref = held
    turn = lax.axis_index("z")
    heads = [lax.rem(turn + j, HEADS) for j in SENDS]
    columns = [pl.ds(pl.multiple_of(h * DH, DH), DH) for h in heads]
    copies[0].wait()
    copies[1].wait()
    for out, cols in zip(outs, columns):
        out[:, :DH] = norm(k_ref[:, cols].astype(F32), kg_ref[:, cols]).astype(BF)
    copies[2].wait()
    for out, cols in zip(outs, columns):
        out[:, DH : 2 * DH] = v_ref[:, cols]
    copies[3].wait()
    copies[4].wait()
    for out, cols in zip(outs, columns):
        queries = norm(q_ref[:, cols].astype(F32), qg_ref[:, cols])
        out[:, 2 * DH :] = (queries * (1.0 / math.sqrt(DH))).astype(BF)


def norms(*arrays):
    return pl.pallas_call(
        norm_kernel,
        out_shape=[jax.ShapeDtypeStruct((ROWS, 3 * DH), BF)] * HEADS,
        in_specs=[ANY] * 5,
        out_specs=[VM] * HEADS,
        scratch_shapes=[pltpu.VMEM(a.shape, a.dtype) for a in arrays]
        + [pltpu.SemaphoreType.DMA((5,))],
        compiler_params=pltpu.CompilerParams(vmem_limit_bytes=62 << 20),
    )(*arrays)


def flash_kernel(first, last, nq, nkv, most, *refs):
    queries, refs = refs[:nq], refs[nq:]
    pieces, refs = refs[:nkv], refs[nkv:]
    if not first:
        (acc_in, max_in, sum_in), refs = refs[:3], refs[3:]
    outs = refs
    blocks, size = [[]], 0
    for p in pieces:
        if size + p.shape[0] > most and blocks[-1]:
            blocks.append([])
            size = 0
        blocks[-1].append(p)
        size += p.shape[0]
    for i in range(nq):
        rows = slice(i * ROWS, (i + 1) * ROWS)
        q = queries[i][:, 2 * DH :]

        def scores(block):
            keys = jnp.concatenate([p[:, :DH] for p in block], axis=0)
            return lax.dot_general(q, keys, NT, preferred_element_type=F32)

        if first:
            high = None
        else:
            high, total, acc = max_in[rows, :1], sum_in[rows, :1], acc_in[rows, :]
        ahead = scores(blocks[0])
        for b, block in enumerate(blocks):
            s = ahead
            if b + 1 < len(blocks):
                ahead = scores(blocks[b + 1])
            top = jnp.max(s, axis=1, keepdims=True)
            top = top if high is None else jnp.maximum(high, top)
            weights = jnp.exp(s - top).astype(BF)
            values = jnp.concatenate([p[:, DH : 2 * DH] for p in block], axis=0)
            both = jnp.dot(
                weights,
                jnp.concatenate([values, jnp.ones_like(values)], axis=1),
                preferred_element_type=F32,
            )
            part, psum = both[:, :DH], both[:, DH : DH + 1]
            if high is None:
                acc, total = part, psum
            else:
                scale = jnp.exp(high - top)
                acc, total = acc * scale + part, total * scale + psum
            high = top
        if last:
            outs[i][...] = (acc / total).astype(BF)
        else:
            outs[0][rows, :] = acc
            outs[1][rows, :] = jnp.broadcast_to(high, (ROWS, DH))
            outs[2][rows, :] = jnp.broadcast_to(total, (ROWS, DH))


def flash(last, queries, pieces, state=(), most=2304):
    n, nq = len(pieces), len(queries)
    if last:
        shapes = [jax.ShapeDtypeStruct((ROWS, DH), BF)] * nq
    else:
        shapes = [jax.ShapeDtypeStruct((nq * ROWS, DH), F32)] * 3
    return pl.pallas_call(
        functools.partial(flash_kernel, not state, last, nq, n, most),
        out_shape=shapes,
        in_specs=[VM] * (nq + n + len(state)),
        out_specs=[VM] * len(shapes),
        compiler_params=pltpu.CompilerParams(vmem_limit_bytes=VLIM),
        cost_estimate=pl.CostEstimate(flops=1000, bytes_accessed=1000, transcendentals=0),
    )(*queries, *pieces, *state)


def project_kernel(steps, first, last, w_hbm, *refs):
    n = len(steps)
    blocks, refs = refs[:n], refs[n:]
    acc_ref, refs = refs[0], refs[1:]
    out_ref, weight, tokens, sems = refs
    halves = range(2) if last is None else (last,)
    used = slice(halves[0] * HALF, (halves[-1] + 1) * HALF)
    turn, col, core = [lax.axis_index(a) for a in ("z", "col", "row")]
    wide = HEADS * DH
    copies = []
    for k, s in enumerate(steps):
        source = lax.rem(col + NY - s, NY)
        rows = pl.ds(pl.multiple_of(source * wide, wide), wide)
        copies.append(pltpu.make_async_copy(w_hbm.at[rows], weight.at[k], sems.at[k]))
    for c in copies:
        c.start()
    for k in range(n):
        for j in range(HEADS):
            head = lax.rem(turn + SENDS[j], HEADS)
            cols = pl.ds(pl.multiple_of(head * DH, DH), DH)
            for i in halves:
                rows = pl.ds(pl.multiple_of(lax.rem(core + i, 2) * HALF, 16), HALF)
                tokens[k, i * HALF : (i + 1) * HALF, cols] = blocks[k][rows, j * DH : (j + 1) * DH]
    for c in copies:
        c.wait()
    total = None if first else acc_ref[used, :]
    for k in range(n):
        part = jnp.dot(tokens[k, used, :], weight[k], preferred_element_type=F32)
        total = part if total is None else total + part
    if first:
        out_ref[:HALF, :] = acc_ref[...].astype(F32) + total[:HALF]
        out_ref[HALF:, :] = total[HALF:]
    else:
        out_ref[...] = total.astype(out_ref.dtype)


def project(steps, first, last, weight, blocks, total):
    n = len(steps)
    wide, width = HEADS * DH, weight.shape[1]
    if last is None:
        shape = jax.ShapeDtypeStruct((ROWS, width), F32)
    else:
        shape = jax.ShapeDtypeStruct((HALF, width), BF if last else F32)
    return pl.pallas_call(
        functools.partial(project_kernel, steps, first, last),
        out_shape=shape,
        in_specs=[ANY] + [VM] * (n + 1),
        out_specs=VM,
        scratch_shapes=[
            pltpu.VMEM((n, wide, width), BF),
            pltpu.VMEM((n, ROWS, wide), BF),
            pltpu.SemaphoreType.DMA((n,)),
        ],
        compiler_params=pltpu.CompilerParams(vmem_limit_bytes=VLIM),
    )(weight, *blocks, total)


def owner_pairs(j):
    return [
        (z * NC + c, (HEADS * c + (z + SENDS[j]) % HEADS) * NC + z // HEADS)
        for z in range(NZ)
        for c in range(NC)
    ]


def to_owner(value, j):
    return lax.ppermute(value, ("z", "row"), owner_pairs(j))


def from_owner(value, j):
    return lax.ppermute(value, ("z", "row"), [(b, a) for a, b in owner_pairs(j)])


def shift(value, axis, size, step):
    if step == 0:
        return value
    return lax.ppermute(value, axis, [(i, (i + step) % size) for i in range(size)])


def swap(value):
    return lax.ppermute(value, "row", [(0, 1), (1, 0)])


def body(query_proj, key_proj, value_proj, query_gain, key_gain, residual, out_weight):
    ready = norms(
        key_proj, key_gain.reshape(1, -1), value_proj, query_proj, query_gain.reshape(1, -1)
    )
    held = [to_owner(ready[j], j) for j in range(HEADS)]
    own = jnp.concatenate([m[:, : 2 * DH] for m in held], axis=0)
    near, back = shift(own, "x", NX, 1), shift(own, "x", NX, -1)
    half = own.shape[0] // 2
    state = flash(False, held, [own, swap(own[:half]), swap(own[half:])])
    half = own.shape[0] // 2
    far = [shift(near[:half], "x", NX, 1), shift(back[half:], "x", NX, -1)]
    near, back, *state = lax.optimization_barrier((near, back, *state))
    state = flash(False, held, [near, back, swap(near), swap(back)], state)
    *far, a, b, c = lax.optimization_barrier((*far, *state))
    attended = flash(True, held, far + [swap(p) for p in far], (a, b, c))
    mine = jnp.concatenate([from_owner(attended[j], j) for j in range(HEADS)], axis=1)
    far, near, back = [shift(mine, "col", NY, s) for s in (2, 1, 3)]
    total = project((0,), True, None, out_weight, [mine], residual)
    near, back, total = lax.optimization_barrier((near, back, total))
    total = project((1, 3), False, None, out_weight, [near, back], total)
    far, total = lax.optimization_barrier((far, total))
    send = swap(project((2,), False, 1, out_weight, [far], total))
    keep = project((2,), False, 0, out_weight, [far], total)
    return (keep + send.astype(F32)).astype(BF)


def solution(mesh):
    fine = Mesh(mesh.devices.reshape(NZ, NX, NC, NY), ("z", "x", "row", "col"))
    seq = ("z", "x")
    heads = ("row", "col")
    placed = (
        P(seq, heads),
        P(seq, heads),
        P(seq, heads),
        P(heads),
        P(heads),
        P(("z", "x", "row"), "col"),
        P("row", "col"),
    )
    return jax.shard_map(
        body, mesh=fine, in_specs=placed, out_specs=P(("z", "x", "row"), "col"), check_vma=False
    )
```
